32 devices in a mesh: groups: 2 (over y), rows: 4 (over z), cols: 2 (over x), rhs: 2 (over core).
Axes of the slice: x: 2, y: 2, z: 4, core: 2. Of those that a mesh axis runs over, the one named last changes fastest.
Arguments:
- later_solution: bfloat16 [10240, 1024], P(('groups', 'rows', 'cols'), 'rhs'), parts along dimension 0, may hold values from -6 to 6
- factor_panel: bfloat16 [10240, 4, 2048], P(('groups', 'rows'), None, 'cols'), parts along dimension 0, may hold values from -0.078125 to 0.078125
- coupling: bfloat16 [12, 2048, 2048], P('groups', 'rows', 'cols'), parts along dimension 0, may hold values from -0.125 to 0.125
- inverse_diag: bfloat16 [8, 2048, 2048], P('groups', 'rows', 'cols'), parts along dimension 0, as said below
- right_side: bfloat16 [8, 2048, 1024], P('groups', 'cols', 'rhs'), parts along dimension 0, may hold values from -6 to 6
Outputs:
- window_solution: bfloat16 [8, 2048, 1024], P('groups', ('rows', 'cols'), 'rhs'), parts along dimension 0
The draws below stay inside these ranges and needn't reach their ends.
There are 2 independent parts, one for each index of `groups`. The reference program is written for one: setup_inputs(seed, part) draws one part's arguments, and reference() takes and returns one part's arrays. A program takes and returns all parts, laid end to end along the dimension named above; each array names one. Nothing has to cross between parts.
Inputs may be any that keep to these rules, and one draw needn't show every extreme that they name: Each inverse_diag[k] is upper triangular (zero below its diagonal) with a positive diagonal.
All inputs are finite; a program needn't handle non-finite values.
Results may differ from the reference program's by a relative error of at most 0.0073.
Values may be sent and summed in bfloat16 or wider, within the bound.
A program may use at most 128 MiB of HBM per device.

```python
import math
import jax
import jax.numpy as jnp
from jax import lax

NB = 2048
W = 4
R = 1024
LATER = 5120
NPAIR = 6


def draw_inverse_diag(key, part):
    key = jax.random.fold_in(key, 11)
    off_key, diag_key = jax.random.split(key)
    full_shape = (W, NB, NB)
    row_ids = lax.broadcasted_iota(jnp.int32, full_shape, 1)
    col_ids = lax.broadcasted_iota(jnp.int32, full_shape, 2)
    above_diag = jax.random.normal(off_key, full_shape, jnp.float32) * (0.7 / math.sqrt(NB))
    diagonal = jax.random.uniform(diag_key, full_shape, jnp.float32, 0.6, 1.4)
    values = jnp.where(col_ids > row_ids, above_diag, jnp.where(col_ids == row_ids, diagonal, 0.0))
    return values.astype(jnp.bfloat16)


def block_levels(stream_key, dims, cuts, least, largest):
    def one(position, parts):
        steps = jax.random.uniform(jax.random.fold_in(jax.random.fold_in(stream_key, 6), position), (parts,), jnp.float32, least / len(cuts), largest / len(cuts))
        return jnp.repeat(jnp.exp(steps), dims[position] // parts).reshape((-1,) + (1,) * (len(dims) - position - 1))

    gain = one(*cuts[0])
    for cut in cuts[1:]:
        gain = gain * one(*cut)
    return gain


def centred(own_key, shape, scale, limit, shards=(), held_as=jnp.bfloat16):
    values = jax.random.normal(own_key, shape, jnp.float32) * scale
    if len(shards) > 0:
        values = block_levels(own_key, shape, shards, -0.22, 0.18) * values
    return jnp.clip(values, min=-limit, max=limit).astype(held_as)


def setup_inputs(seed: int = 0, part: int = 0) -> dict:
    arg_keys = jax.random.split(jax.random.key(seed), 6)
    own_keys = jax.random.split(jax.random.fold_in(arg_keys[5], part), 6)
    later_solution = centred(own_keys[0], (LATER, R), 1.0, 6.0, ((0, 8), (1, 2)))
    factor_panel = centred(own_keys[1], (LATER, W, NB), LATER ** -0.5, 0.078125, ((0, 4), (2, 2)))
    coupling = centred(own_keys[2], (NPAIR, NB, NB), NB ** -0.5, 0.125, ((1, 4), (2, 2)))
    inverse_diag = draw_inverse_diag(jax.random.fold_in(jax.random.fold_in(arg_keys[5], part), 71), part)
    right_side = centred(own_keys[4], (W, NB, R), 1.0, 6.0, ((1, 2), (2, 2)))
    return dict(later_solution=later_solution, factor_panel=factor_panel, coupling=coupling, inverse_diag=inverse_diag, right_side=right_side)


def pair_lookup(blocks):
    mapping = {}
    counter = 0
    for current in range(blocks - 2, -1, -1):
        for source in range(current + 1, blocks):
            mapping[(source, current)] = counter
            counter += 1
    return mapping


def reference(later_solution, factor_panel, coupling, inverse_diag, right_side):
    blocks = factor_panel.shape[1]
    lookup = pair_lookup(blocks)
    solved = {}
    for current in range(blocks - 1, -1, -1):
        summed = jnp.dot(factor_panel[:, current, :].T, later_solution, preferred_element_type=jnp.float32)
        for source in range(current + 1, blocks):
            summed = summed + jnp.dot(coupling[lookup[(source, current)]].T, solved[source], preferred_element_type=jnp.float32)
        residual = (right_side[current].astype(jnp.float32) - summed).astype(jnp.bfloat16)
        solved[current] = jnp.dot(inverse_diag[current], residual, preferred_element_type=jnp.float32).astype(jnp.bfloat16)
    return jnp.stack([solved[current] for current in range(blocks)])
```

```python
import functools

import jax
import jax.numpy as jnp
from jax import lax
from jax.experimental import pallas as pl
from jax.experimental.pallas import tpu as pltpu
from jax.sharding import PartitionSpec as P

F32, BF16 = jnp.float32, jnp.bfloat16
MESH = pl.DeviceIdType.MESH
CHUNKS = 4
HOP_LAG = 2
SWAP_LAG = 4
LEAD = 2


def nn(a, b):
    return lax.dot_general(a, b, (((1,), (0,)), ((), ())), preferred_element_type=F32)


def nt(a, b):
    return lax.dot_general(a, b, (((1,), (1,)), ((), ())), preferred_element_type=F32)


def transposed(a):
    return a.astype(F32).T


def kernel(
    nz, nx, chunks, subs,
    later, panel, coup, inv, rhs, out,
    panel_v, coup_v, inv_v, rhs_v, later_v, later_t, acc, from_lo, from_hi, to_hi, to_lo,
    prod, swap_out, swap_in, sol, out_v,
    panel_s, coup_s, inv_s, rhs_s, later_s, out_s,
    gather_ss, gather_rs, hi_ss, lo_ss, lo_rs, hi_rs, swap_ss, swap_rs,
):
    z = lax.axis_index("rows")
    x = lax.axis_index("cols")
    blocks, depth, bc = panel_v.shape
    pairs, _, own, qc = coup_v.shape
    cw = rhs_v.shape[3]
    lr = depth // nx
    piece = own // nx
    last_z = nz - 1
    far = jnp.maximum(z, last_z - z)
    period = max(chunks * subs, subs - 1 + HOP_LAG * last_z + SWAP_LAG)

    barrier = pltpu.get_barrier_semaphore()

    @pl.when(z > 0)
    def _():
        pl.semaphore_signal(barrier, inc=1, device_id={"rows": z - 1}, device_id_type=MESH)

    @pl.when(z < last_z)
    def _():
        pl.semaphore_signal(barrier, inc=1, device_id={"rows": z + 1}, device_id_type=MESH)

    def peer(d):
        return lax.rem(x + d, nx)

    def source(d):
        return lax.rem(x + nx - d, nx)

    for d in range(1, nx):
        pl.semaphore_signal(barrier, inc=1, device_id={"cols": peer(d)}, device_id_type=MESH)

    def load_later(c):
        return pltpu.make_async_copy(
            later.at[:, pl.ds(c * cw, cw)], later_v.at[c, pl.ds(pl.multiple_of(x * lr, 16), lr), :], later_s.at[c])

    def load_panel(i):
        return pltpu.make_async_copy(panel.at[blocks - 1 - i], panel_v.at[i], panel_s.at[i])

    def load_inv(i, q):
        return pltpu.make_async_copy(
            inv.at[blocks - 1 - i, :, pl.ds(q * qc, qc)], inv_v.at[i, q], inv_s.at[i, q])

    def load_rhs(i, c):
        return pltpu.make_async_copy(
            rhs.at[blocks - 1 - i, :, pl.ds(c * cw, cw)], rhs_v.at[i, c], rhs_s.at[i, c])

    def load_coup(p, q):
        return pltpu.make_async_copy(
            coup.at[p, :, pl.ds(q * qc, qc)], coup_v.at[p, q], coup_s.at[p, q])

    for c in range(chunks):
        load_later(c).start()
    load_panel(0).start()

    greeted = (nx - 1) + jnp.where(z > 0, 1, 0) + jnp.where(z < last_z, 1, 0)
    pl.semaphore_wait(barrier, greeted)

    def gather(c, d, who, place):
        return pltpu.make_async_remote_copy(
            src_ref=later.at[:, pl.ds(c * cw, cw)],
            dst_ref=later_v.at[c, pl.ds(pl.multiple_of(place * lr, 16), lr), :],
            send_sem=gather_ss.at[c, d - 1], recv_sem=gather_rs.at[c, d - 1],
            device_id={"cols": who}, device_id_type=MESH)

    for c in range(chunks):
        for d in range(1, nx):
            gather(c, d, peer(d), x).start()

    for i in range(blocks):
        if i > 0:
            load_panel(i).start()
        for q in range(subs):
            load_inv(i, q).start()
        for c in range(chunks):
            load_rhs(i, c).start()
    for p in range(pairs):
        for q in range(subs):
            load_coup(p, q).start()

    @pl.when(z == 0)
    def _():
        @pl.loop(0, blocks * chunks * subs)
        def _(i):
            from_lo[i] = jnp.zeros((cw, qc), BF16)

    @pl.when(z == last_z)
    def _():
        @pl.loop(0, blocks * chunks * subs)
        def _(i):
            from_hi[i] = jnp.zeros((cw, qc), BF16)

    def send_hi(slot, idx):
        return pltpu.make_async_remote_copy(
            src_ref=to_hi.at[slot], dst_ref=from_lo.at[idx],
            send_sem=hi_ss.at[slot], recv_sem=lo_rs.at[idx],
            device_id={"rows": jnp.minimum(z + 1, last_z)}, device_id_type=MESH)

    def send_lo(slot, idx):
        return pltpu.make_async_remote_copy(
            src_ref=to_lo.at[slot], dst_ref=from_hi.at[idx],
            send_sem=lo_ss.at[slot], recv_sem=hi_rs.at[idx],
            device_id={"rows": jnp.maximum(z - 1, 0)}, device_id_type=MESH)

    def swap(i, c, d):
        return pltpu.make_async_remote_copy(
            src_ref=swap_out.at[i, c], dst_ref=swap_in.at[i, c, d - 1],
            send_sem=swap_ss.at[i, c, d - 1], recv_sem=swap_rs.at[i, c, d - 1],
            device_id={"cols": peer(d)}, device_id_type=MESH)

    def store_out(i, c):
        return pltpu.make_async_copy(
            out_v.at[i, c, pl.ds(pl.multiple_of(x * piece, 16), piece), :],
            out.at[blocks - 1 - i, :, pl.ds(pl.multiple_of(c * cw, cw), cw)],
            out_s.at[i, c])

    def decode(tau):
        at = jnp.maximum(tau, 0)
        i = lax.div(at, period)
        r = at - i * period
        valid = (tau >= 0) & (i < blocks) & (r < chunks * subs)
        return valid, i, lax.div(r, subs), lax.rem(r, subs)

    def finish_block(t):
        valid, i, c, q = decode(t - HOP_LAG * far - SWAP_LAG)

        @pl.when(valid & (q == subs - 1))
        def _():
            total = prod[c]
            for d in range(1, nx):
                swap(i, c, d).wait()
                total = total + swap_in[i, c, d - 1].astype(F32)
            sol[c] = total.astype(BF16)

            @pl.loop(i + 1, blocks)
            def _(target):
                p = lax.div(target * (target - 1), 2) + target - 1 - i

                @pl.when(c == 0)
                def _():
                    for s in range(subs):
                        load_coup(p, s).wait()

                for s in range(subs):
                    acc[target, c, s] += nn(sol[c], coup_v[p, s])

            out_v[i, c] = transposed(sol[c]).astype(BF16)
            store_out(i, c).start()

    def flow_hi(t):
        valid, i, c, q = decode(t - HOP_LAG * z)

        @pl.when(valid & (z < last_z))
        def _():
            slot = c * subs + q
            idx = i * (chunks * subs) + slot

            @pl.when(z > 0)
            def _():
                send_hi(slot, idx).wait_recv()

            @pl.when(i > 0)
            def _():
                send_hi(slot, idx).wait_send()

            to_hi[slot] = (acc[i, c, q] + from_lo[idx].astype(F32)).astype(BF16)
            send_hi(slot, idx).start()

    def flow_lo(t):
        valid, i, c, q = decode(t - HOP_LAG * (last_z - z))

        @pl.when(valid & (z > 0))
        def _():
            slot = c * subs + q
            idx = i * (chunks * subs) + slot

            @pl.when(z < last_z)
            def _():
                send_lo(slot, idx).wait_recv()

            @pl.when(i > 0)
            def _():
                send_lo(slot, idx).wait_send()

            to_lo[slot] = (acc[i, c, q] + from_hi[idx].astype(F32)).astype(BF16)
            send_lo(slot, idx).start()

    def diagonal(t):
        valid, i, c, q = decode(t - HOP_LAG * far)

        @pl.when(valid)
        def _():
            slot = c * subs + q
            idx = i * (chunks * subs) + slot

            @pl.when((c == 0) & (q == 0))
            def _():
                for s in range(subs):
                    load_inv(i, s).wait()
                for s in range(chunks):
                    load_rhs(i, s).wait()

            right = transposed(rhs_v[i, c, pl.ds(pl.multiple_of(q * qc, qc), qc), :])

            if nz > 1:
                @pl.when(z == last_z)
                def _():
                    send_hi(slot, idx).wait_recv()

                @pl.when(z == 0)
                def _():
                    send_lo(slot, idx).wait_recv()

            total = acc[i, c, q] + from_lo[idx].astype(F32) + from_hi[idx].astype(F32)
            residual = (right - total).astype(BF16)
            term = nt(residual, inv_v[i, q])

            @pl.when(q == 0)
            def _():
                prod[c] = term

            @pl.when(q > 0)
            def _():
                prod[c] += term

            @pl.when(q == subs - 1)
            def _():
                swap_out[i, c] = prod[c].astype(BF16)
                for d in range(1, nx):
                    swap(i, c, d).start()

    def later_terms(t):
        u = t + LEAD
        c = lax.div(u, subs)
        for j in range(-(-blocks // subs)):
            i = lax.rem(u, subs) + j * subs

            @pl.when((c < chunks) & (i < blocks))
            def _():
                @pl.when(i == 0)
                def _():
                    load_later(c).wait()
                    for d in range(1, nx):
                        gather(c, d, peer(d), source(d)).wait_recv()
                    later_t[c] = transposed(later_v[c]).astype(BF16)

                @pl.when(c == 0)
                def _():
                    load_panel(i).wait()

                for s in range(subs):
                    acc[i, c, s] = nn(later_t[c], panel_v[i, :, s * qc:(s + 1) * qc])

    steps = LEAD + (blocks - 1) * period + chunks * subs + HOP_LAG * last_z + SWAP_LAG

    def tick(u, carry):
        t = u - LEAD
        finish_block(t)
        flow_hi(t)
        flow_lo(t)
        diagonal(t)
        later_terms(t)
        return carry

    lax.fori_loop(0, steps, tick, 0)

    for c in range(chunks):
        for d in range(1, nx):
            gather(c, d, peer(d), x).wait_send()

    @pl.when(z < last_z)
    def _():
        @pl.loop(0, chunks * subs)
        def _(slot):
            send_hi(slot, slot).wait_send()

    @pl.when(z > 0)
    def _():
        @pl.loop(0, chunks * subs)
        def _(slot):
            send_lo(slot, slot).wait_send()

    for i in range(blocks):
        for c in range(chunks):
            store_out(i, c).wait()


def on_device(nz, nx, later_solution, factor_panel, coupling, inverse_diag, right_side):
    depth, blocks, bc = factor_panel.shape
    rhs_cols = later_solution.shape[1]
    pairs, own, _ = coupling.shape
    subs = max(1, min(4, bc // 128))
    chunks = CHUNKS
    cw, qc = rhs_cols // chunks, bc // subs
    per_block = chunks * subs
    others = max(nx - 1, 1)
    panel = jnp.transpose(factor_panel, (1, 0, 2))
    dma = pltpu.SemaphoreType.DMA
    vmem = pltpu.VMEM
    flops = 2 * rhs_cols * bc * (depth * blocks + own * (pairs + blocks))
    return pl.pallas_call(
        functools.partial(kernel, nz, nx, chunks, subs),
        out_shape=jax.ShapeDtypeStruct((blocks, own // nx, rhs_cols), BF16),
        in_specs=[pl.BlockSpec(memory_space=pl.ANY)] * 5,
        out_specs=pl.BlockSpec(memory_space=pl.ANY),
        scratch_shapes=[
            vmem((blocks, depth, bc), BF16),
            vmem((pairs, subs, own, qc), BF16),
            vmem((blocks, subs, own, qc), BF16),
            vmem((blocks, chunks, bc, cw), BF16),
            vmem((chunks, depth, cw), BF16),
            vmem((chunks, cw, depth), BF16),
            vmem((blocks, chunks, subs, cw, qc), F32),
            vmem((blocks * per_block, cw, qc), BF16),
            vmem((blocks * per_block, cw, qc), BF16),
            vmem((per_block, cw, qc), BF16),
            vmem((per_block, cw, qc), BF16),
            vmem((chunks, cw, own), F32),
            vmem((blocks, chunks, cw, own), BF16),
            vmem((blocks, chunks, others, cw, own), BF16),
            vmem((chunks, cw, own), BF16),
            vmem((blocks, chunks, own, cw), BF16),
            dma((blocks,)), dma((pairs, subs)), dma((blocks, subs)), dma((blocks, chunks)),
            dma((chunks,)), dma((blocks, chunks)),
            dma((chunks, others)), dma((chunks, others)),
            dma((per_block,)), dma((per_block,)),
            dma((blocks * per_block,)), dma((blocks * per_block,)),
            dma((blocks, chunks, others)), dma((blocks, chunks, others)),
        ],
        compiler_params=pltpu.CompilerParams(
            collective_id=0, has_side_effects=True, vmem_limit_bytes=60 * 2**20),
        cost_estimate=pl.CostEstimate(
            flops=flops, bytes_accessed=2 * (depth * blocks * bc + own * bc * (pairs + blocks)), transcendentals=0),
    )(later_solution, panel, coupling, inverse_diag, right_side)


def solution(mesh):
    placed = (
        P(("groups", "rows", "cols"), "rhs"),
        P(("groups", "rows"), None, "cols"),
        P("groups", "rows", "cols"),
        P("groups", "rows", "cols"),
        P("groups", "cols", "rhs"),
    )
    return jax.shard_map(
        functools.partial(on_device, mesh.shape["rows"], mesh.shape["cols"]),
        mesh=mesh,
        in_specs=placed,
        out_specs=P("groups", ("rows", "cols"), "rhs"),
        check_vma=False,
    )
```

```python
import functools

import jax
import jax.numpy as jnp
from jax import lax
from jax.experimental import pallas as pl
from jax.experimental.pallas import tpu as pltpu
from jax.sharding import PartitionSpec as P

F32, BF16 = jnp.float32, jnp.bfloat16
MESH = pl.DeviceIdType.MESH
CHUNKS = 4
SUBS = 4
HOP_LAG = 3
SWAP_LAG = 5
LEAD = 1


def nn(a, b):
    return lax.dot_general(a, b, (((1,), (0,)), ((), ())), preferred_element_type=F32)


def nt(a, b):
    return lax.dot_general(a, b, (((1,), (1,)), ((), ())), preferred_element_type=F32)


def transposed(a):
    return a.astype(F32).T


def kernel(
    nz, nx, chunks, subs,
    later, panel, coup, inv, rhs, out,
    panel_v, coup_v, inv_v, rhs_v, later_v, later_t, acc, from_lo, from_hi, to_hi, to_lo,
    prod, swap_out, swap_in, sol, out_v,
    panel_s, coup_s, inv_s, rhs_s, later_s, out_s,
    gather_ss, gather_rs, hi_ss, lo_ss, lo_rs, hi_rs, swap_ss, swap_rs,
):
    z = lax.axis_index("rows")
    x = lax.axis_index("cols")
    blocks, depth, bc = panel_v.shape
    pairs, _, own, qc = coup_v.shape
    cw = rhs_v.shape[3]
    lr = depth // nx
    piece = own // nx
    last_z = nz - 1
    far = jnp.maximum(z, last_z - z)
    period = max(chunks * subs, subs - 1 + HOP_LAG * last_z + SWAP_LAG)

    barrier = pltpu.get_barrier_semaphore()

    @pl.when(z > 0)
    def _():
        pl.semaphore_signal(barrier, inc=1, device_id={"rows": z - 1}, device_id_type=MESH)

    @pl.when(z < last_z)
    def _():
        pl.semaphore_signal(barrier, inc=1, device_id={"rows": z + 1}, device_id_type=MESH)

    def peer(d):
        return lax.rem(x + d, nx)

    def source(d):
        return lax.rem(x + nx - d, nx)

    for d in range(1, nx):
        pl.semaphore_signal(barrier, inc=1, device_id={"cols": peer(d)}, device_id_type=MESH)

    def load_later(c):
        return pltpu.make_async_copy(
            later.at[:, pl.ds(c * cw, cw)], later_v.at[c, pl.ds(pl.multiple_of(x * lr, 16), lr), :], later_s.at[c])

    def load_panel(i):
        return pltpu.make_async_copy(panel.at[blocks - 1 - i], panel_v.at[i], panel_s.at[i])

    def load_inv(i, q):
        return pltpu.make_async_copy(
            inv.at[blocks - 1 - i, :, pl.ds(q * qc, qc)], inv_v.at[i, q], inv_s.at[i, q])

    def load_rhs(i, c):
        return pltpu.make_async_copy(
            rhs.at[blocks - 1 - i, :, pl.ds(c * cw, cw)], rhs_v.at[i, c], rhs_s.at[i, c])

    def load_coup(p, q):
        return pltpu.make_async_copy(
            coup.at[p, :, pl.ds(q * qc, qc)], coup_v.at[p, q], coup_s.at[p, q])

    for c in range(chunks):
        load_later(c).start()
    load_panel(0).start()

    greeted = (nx - 1) + jnp.where(z > 0, 1, 0) + jnp.where(z < last_z, 1, 0)
    pl.semaphore_wait(barrier, greeted)

    def gather(c, d, who, place):
        return pltpu.make_async_remote_copy(
            src_ref=later.at[:, pl.ds(c * cw, cw)],
            dst_ref=later_v.at[c, pl.ds(pl.multiple_of(place * lr, 16), lr), :],
            send_sem=gather_ss.at[c, d - 1], recv_sem=gather_rs.at[c, d - 1],
            device_id={"cols": who}, device_id_type=MESH)

    for c in range(chunks):
        for d in range(1, nx):
            gather(c, d, peer(d), x).start()

    for i in range(blocks):
        if i > 0:
            load_panel(i).start()
        for q in range(subs):
            load_inv(i, q).start()
        for c in range(chunks):
            load_rhs(i, c).start()
    for p in range(pairs):
        for q in range(subs):
            load_coup(p, q).start()

    @pl.when(z == 0)
    def _():
        @pl.loop(0, blocks * chunks * subs)
        def _(i):
            from_lo[i] = jnp.zeros((cw, qc), BF16)

    @pl.when(z == last_z)
    def _():
        @pl.loop(0, blocks * chunks * subs)
        def _(i):
            from_hi[i] = jnp.zeros((cw, qc), BF16)

    def send_hi(slot, idx):
        return pltpu.make_async_remote_copy(
            src_ref=to_hi.at[slot], dst_ref=from_lo.at[idx],
            send_sem=hi_ss.at[slot], recv_sem=lo_rs.at[idx],
            device_id={"rows": jnp.minimum(z + 1, last_z)}, device_id_type=MESH)

    def send_lo(slot, idx):
        return pltpu.make_async_remote_copy(
            src_ref=to_lo.at[slot], dst_ref=from_hi.at[idx],
            send_sem=lo_ss.at[slot], recv_sem=hi_rs.at[idx],
            device_id={"rows": jnp.maximum(z - 1, 0)}, device_id_type=MESH)

    def swap(i, c, d):
        return pltpu.make_async_remote_copy(
            src_ref=swap_out.at[i, c], dst_ref=swap_in.at[i, c, d - 1],
            send_sem=swap_ss.at[i, c, d - 1], recv_sem=swap_rs.at[i, c, d - 1],
            device_id={"cols": peer(d)}, device_id_type=MESH)

    def store_out(i, c):
        return pltpu.make_async_copy(
            out_v.at[i, c, pl.ds(pl.multiple_of(x * piece, 16), piece), :],
            out.at[blocks - 1 - i, :, pl.ds(pl.multiple_of(c * cw, cw), cw)],
            out_s.at[i, c])

    def decode(tau):
        at = jnp.maximum(tau, 0)
        i = lax.div(at, period)
        r = at - i * period
        valid = (tau >= 0) & (i < blocks) & (r < chunks * subs)
        return valid, i, lax.div(r, subs), lax.rem(r, subs)

    def finish_block(t):
        valid, i, c, q = decode(t - HOP_LAG * far - SWAP_LAG)

        @pl.when(valid & (q == subs - 1))
        def _():
            total = prod[c]
            for d in range(1, nx):
                swap(i, c, d).wait()
                total = total + swap_in[i, c, d - 1].astype(F32)
            sol[c] = total.astype(BF16)

            @pl.when(i + 1 < blocks)
            def _():
                couple(i, c, i + 1)

    def couple(i, c, target):
        p = lax.div(target * (target - 1), 2) + target - 1 - i

        @pl.when(c == 0)
        def _():
            for s in range(subs):
                load_coup(p, s).wait()

        for s in range(subs):
            acc[target, c, s] += nn(sol[c], coup_v[p, s])

    def rest_of_block(t):
        for delta in range(1, blocks - 1):
            valid, i, c, q = decode(t - HOP_LAG * far - SWAP_LAG - delta)

            @pl.when(valid & (q == subs - 1))
            def _():
                if delta == 1:
                    out_v[i, c] = transposed(sol[c]).astype(BF16)
                    store_out(i, c).start()

                @pl.when(i + 1 + delta < blocks)
                def _():
                    couple(i, c, i + 1 + delta)

    def flow_hi(t):
        valid, i, c, q = decode(t - HOP_LAG * z)

        @pl.when(valid & (z < last_z))
        def _():
            slot = c * subs + q
            idx = i * (chunks * subs) + slot

            @pl.when(z > 0)
            def _():
                send_hi(slot, idx).wait_recv()

            @pl.when(i > 0)
            def _():
                send_hi(slot, idx).wait_send()

            to_hi[slot] = (acc[i, c, q] + from_lo[idx].astype(F32)).astype(BF16)
            send_hi(slot, idx).start()

    def flow_lo(t):
        valid, i, c, q = decode(t - HOP_LAG * (last_z - z))

        @pl.when(valid & (z > 0))
        def _():
            slot = c * subs + q
            idx = i * (chunks * subs) + slot

            @pl.when(z < last_z)
            def _():
                send_lo(slot, idx).wait_recv()

            @pl.when(i > 0)
            def _():
                send_lo(slot, idx).wait_send()

            to_lo[slot] = (acc[i, c, q] + from_hi[idx].astype(F32)).astype(BF16)
            send_lo(slot, idx).start()

    def diagonal(t):
        valid, i, c, q = decode(t - HOP_LAG * far)

        @pl.when(valid)
        def _():
            slot = c * subs + q
            idx = i * (chunks * subs) + slot

            @pl.when((c == 0) & (q == 0))
            def _():
                for s in range(subs):
                    load_inv(i, s).wait()
                for s in range(chunks):
                    load_rhs(i, s).wait()

            right = transposed(rhs_v[i, c, pl.ds(pl.multiple_of(q * qc, qc), qc), :])

            if nz > 1:
                @pl.when(z == last_z)
                def _():
                    send_hi(slot, idx).wait_recv()

                @pl.when(z == 0)
                def _():
                    send_lo(slot, idx).wait_recv()

            total = acc[i, c, q] + from_lo[idx].astype(F32) + from_hi[idx].astype(F32)
            residual = (right - total).astype(BF16)
            term = nt(residual, inv_v[i, q])

            @pl.when(q == 0)
            def _():
                prod[c] = term

            @pl.when(q > 0)
            def _():
                prod[c] += term

            @pl.when(q == subs - 1)
            def _():
                swap_out[i, c] = prod[c].astype(BF16)
                for d in range(1, nx):
                    swap(i, c, d).start()

    def later_terms(t):
        u = t + LEAD
        c = lax.div(u, subs)
        for j in range(-(-blocks // subs)):
            i = lax.rem(u, subs) + j * subs

            @pl.when((c < chunks) & (i < blocks))
            def _():
                @pl.when(i == 0)
                def _():
                    load_later(c).wait()
                    for d in range(1, nx):
                        gather(c, d, peer(d), source(d)).wait_recv()
                    later_t[c] = transposed(later_v[c]).astype(BF16)

                @pl.when(c == 0)
                def _():
                    load_panel(i).wait()

                for s in range(subs):
                    acc[i, c, s] = nn(later_t[c], panel_v[i, :, s * qc:(s + 1) * qc])

    steps = LEAD + (blocks - 1) * period + chunks * subs + HOP_LAG * last_z + SWAP_LAG + 1

    def tick(u, carry):
        t = u - LEAD
        finish_block(t)
        flow_hi(t)
        flow_lo(t)
        diagonal(t)
        rest_of_block(t)
        later_terms(t)
        return carry

    lax.fori_loop(0, steps, tick, 0)

    for c in range(chunks):
        for d in range(1, nx):
            gather(c, d, peer(d), x).wait_send()

    @pl.when(z < last_z)
    def _():
        @pl.loop(0, chunks * subs)
        def _(slot):
            send_hi(slot, slot).wait_send()

    @pl.when(z > 0)
    def _():
        @pl.loop(0, chunks * subs)
        def _(slot):
            send_lo(slot, slot).wait_send()

    for i in range(blocks):
        for c in range(chunks):
            store_out(i, c).wait()


def on_device(nz, nx, later_solution, factor_panel, coupling, inverse_diag, right_side):
    depth, blocks, bc = factor_panel.shape
    rhs_cols = later_solution.shape[1]
    pairs, own, _ = coupling.shape
    subs = max(1, min(SUBS, bc // 128))
    chunks = CHUNKS
    cw, qc = rhs_cols // chunks, bc // subs
    per_block = chunks * subs
    others = max(nx - 1, 1)
    panel = jnp.transpose(factor_panel, (1, 0, 2))
    dma = pltpu.SemaphoreType.DMA
    vmem = pltpu.VMEM
    flops = 2 * rhs_cols * bc * (depth * blocks + own * (pairs + blocks))
    return pl.pallas_call(
        functools.partial(kernel, nz, nx, chunks, subs),
        out_shape=jax.ShapeDtypeStruct((blocks, own // nx, rhs_cols), BF16),
        in_specs=[pl.BlockSpec(memory_space=pl.ANY)] * 5,
        out_specs=pl.BlockSpec(memory_space=pl.ANY),
        scratch_shapes=[
            vmem((blocks, depth, bc), BF16),
            vmem((pairs, subs, own, qc), BF16),
            vmem((blocks, subs, own, qc), BF16),
            vmem((blocks, chunks, bc, cw), BF16),
            vmem((chunks, depth, cw), BF16),
            vmem((chunks, cw, depth), BF16),
            vmem((blocks, chunks, subs, cw, qc), F32),
            vmem((blocks * per_block, cw, qc), BF16),
            vmem((blocks * per_block, cw, qc), BF16),
            vmem((per_block, cw, qc), BF16),
            vmem((per_block, cw, qc), BF16),
            vmem((chunks, cw, own), F32),
            vmem((blocks, chunks, cw, own), BF16),
            vmem((blocks, chunks, others, cw, own), BF16),
            vmem((chunks, cw, own), BF16),
            vmem((blocks, chunks, own, cw), BF16),
            dma((blocks,)), dma((pairs, subs)), dma((blocks, subs)), dma((blocks, chunks)),
            dma((chunks,)), dma((blocks, chunks)),
            dma((chunks, others)), dma((chunks, others)),
            dma((per_block,)), dma((per_block,)),
            dma((blocks * per_block,)), dma((blocks * per_block,)),
            dma((blocks, chunks, others)), dma((blocks, chunks, others)),
        ],
        compiler_params=pltpu.CompilerParams(
            collective_id=0, has_side_effects=True, vmem_limit_bytes=60 * 2**20),
        cost_estimate=pl.CostEstimate(
            flops=flops, bytes_accessed=2 * (depth * blocks * bc + own * bc * (pairs + blocks)), transcendentals=0),
    )(later_solution, panel, coupling, inverse_diag, right_side)


def solution(mesh):
    placed = (
        P(("groups", "rows", "cols"), "rhs"),
        P(("groups", "rows"), None, "cols"),
        P("groups", "rows", "cols"),
        P("groups", "rows", "cols"),
        P("groups", "cols", "rhs"),
    )
    return jax.shard_map(
        functools.partial(on_device, mesh.shape["rows"], mesh.shape["cols"]),
        mesh=mesh,
        in_specs=placed,
        out_specs=P("groups", ("rows", "cols"), "rhs"),
        check_vma=False,
    )
```

```python
import functools

import jax
import jax.numpy as jnp
from jax import lax
from jax.experimental import pallas as pl
from jax.experimental.pallas import tpu as pltpu
from jax.sharding import PartitionSpec as P

F32, BF16 = jnp.float32, jnp.bfloat16
MESH = pl.DeviceIdType.MESH
CHUNKS = 4
SUBS = 4
HOP_LAG = 3
SWAP_LAG = 5
LEAD = 1


def nn(a, b):
    return lax.dot_general(a, b, (((1,), (0,)), ((), ())), preferred_element_type=F32)


def nt(a, b):
    return lax.dot_general(a, b, (((1,), (1,)), ((), ())), preferred_element_type=F32)


def transposed(a):
    return a.astype(F32).T


def kernel(
    nz, nx, chunks, subs,
    later, panel, coup, inv, rhs, out,
    panel_v, coup_v, inv_v, rhs_v, later_v, later_t, acc, from_lo, from_hi, to_hi, to_lo,
    prod, swap_out, swap_in, sol, out_v,
    panel_s, coup_s, inv_s, rhs_s, later_s, out_s,
    gather_ss, gather_rs, hi_ss, lo_ss, lo_rs, hi_rs, swap_ss, swap_rs,
):
    z = lax.axis_index("rows")
    x = lax.axis_index("cols")
    blocks, depth, bc = panel_v.shape
    pairs, _, own, qc = coup_v.shape
    cw = rhs_v.shape[3]
    lr = depth // nx
    piece = own // nx
    last_z = nz - 1
    far = jnp.maximum(z, last_z - z)
    period = max(chunks * subs, subs - 1 + HOP_LAG * last_z + SWAP_LAG)

    def used(row, col, q):
        return col * bc + (q + 1) * qc > row * own

    barrier = pltpu.get_barrier_semaphore()

    @pl.when(z > 0)
    def _():
        pl.semaphore_signal(barrier, inc=1, device_id={"rows": z - 1}, device_id_type=MESH)

    @pl.when(z < last_z)
    def _():
        pl.semaphore_signal(barrier, inc=1, device_id={"rows": z + 1}, device_id_type=MESH)

    def peer(d):
        return lax.rem(x + d, nx)

    def source(d):
        return lax.rem(x + nx - d, nx)

    for d in range(1, nx):
        pl.semaphore_signal(barrier, inc=1, device_id={"cols": peer(d)}, device_id_type=MESH)

    def load_later(c):
        return pltpu.make_async_copy(
            later.at[:, pl.ds(c * cw, cw)], later_v.at[c, pl.ds(pl.multiple_of(x * lr, 16), lr), :], later_s.at[c])

    def load_panel(i):
        return pltpu.make_async_copy(panel.at[blocks - 1 - i], panel_v.at[i], panel_s.at[i])

    def load_inv(i, q):
        return pltpu.make_async_copy(
            inv.at[blocks - 1 - i, :, pl.ds(q * qc, qc)], inv_v.at[i, q], inv_s.at[i, q])

    def load_rhs(i, c):
        return pltpu.make_async_copy(
            rhs.at[blocks - 1 - i, :, pl.ds(c * cw, cw)], rhs_v.at[i, c], rhs_s.at[i, c])

    def load_coup(p, q):
        return pltpu.make_async_copy(
            coup.at[p, :, pl.ds(q * qc, qc)], coup_v.at[p, q], coup_s.at[p, q])

    for c in range(chunks):
        load_later(c).start()
    load_panel(0).start()

    greeted = (nx - 1) + jnp.where(z > 0, 1, 0) + jnp.where(z < last_z, 1, 0)
    pl.semaphore_wait(barrier, greeted)

    def gather(c, d, who, place):
        return pltpu.make_async_remote_copy(
            src_ref=later.at[:, pl.ds(c * cw, cw)],
            dst_ref=later_v.at[c, pl.ds(pl.multiple_of(place * lr, 16), lr), :],
            send_sem=gather_ss.at[c, d - 1], recv_sem=gather_rs.at[c, d - 1],
            device_id={"cols": who}, device_id_type=MESH)

    for c in range(chunks):
        for d in range(1, nx):
            gather(c, d, peer(d), x).start()

    for i in range(blocks):
        if i > 0:
            load_panel(i).start()
        for q in range(subs):
            load_inv(i, q).start()
        for c in range(chunks):
            load_rhs(i, c).start()
    for p in range(pairs):
        for q in range(subs):
            load_coup(p, q).start()

    @pl.when(z == 0)
    def _():
        @pl.loop(0, blocks * chunks * subs)
        def _(i):
            from_lo[i] = jnp.zeros((cw, qc), BF16)

    @pl.when(z == last_z)
    def _():
        @pl.loop(0, blocks * chunks * subs)
        def _(i):
            from_hi[i] = jnp.zeros((cw, qc), BF16)

    def send_hi(slot, idx):
        return pltpu.make_async_remote_copy(
            src_ref=to_hi.at[slot], dst_ref=from_lo.at[idx],
            send_sem=hi_ss.at[slot], recv_sem=lo_rs.at[idx],
            device_id={"rows": jnp.minimum(z + 1, last_z)}, device_id_type=MESH)

    def send_lo(slot, idx):
        return pltpu.make_async_remote_copy(
            src_ref=to_lo.at[slot], dst_ref=from_hi.at[idx],
            send_sem=lo_ss.at[slot], recv_sem=hi_rs.at[idx],
            device_id={"rows": jnp.maximum(z - 1, 0)}, device_id_type=MESH)

    def swap(i, c, d):
        return pltpu.make_async_remote_copy(
            src_ref=swap_out.at[i, c], dst_ref=swap_in.at[i, c, d - 1],
            send_sem=swap_ss.at[i, c, d - 1], recv_sem=swap_rs.at[i, c, d - 1],
            device_id={"cols": peer(d)}, device_id_type=MESH)

    def store_out(i, c):
        return pltpu.make_async_copy(
            out_v.at[i, c, pl.ds(pl.multiple_of(x * piece, 16), piece), :],
            out.at[blocks - 1 - i, :, pl.ds(pl.multiple_of(c * cw, cw), cw)],
            out_s.at[i, c])

    def decode(tau):
        at = jnp.maximum(tau, 0)
        i = lax.div(at, period)
        r = at - i * period
        valid = (tau >= 0) & (i < blocks) & (r < chunks * subs)
        return valid, i, lax.div(r, subs), lax.rem(r, subs)

    def finish_block(t):
        valid, i, c, q = decode(t - HOP_LAG * far - SWAP_LAG)

        @pl.when(valid & (q == subs - 1))
        def _():
            for d in range(1, nx):
                @pl.when(used(z, x, subs - 1))
                def _():
                    swap(i, c, d).wait_send()

                @pl.when(used(z, source(d), subs - 1))
                def _():
                    swap(i, c, d).wait_recv()
                    prod[c] += swap_in[i, c, d - 1].astype(F32)

            sol[c] = prod[c].astype(BF16)

            @pl.when(i + 1 < blocks)
            def _():
                couple(i, c, i + 1)

    def couple(i, c, target):
        p = lax.div(target * (target - 1), 2) + target - 1 - i

        @pl.when(c == 0)
        def _():
            for s in range(subs):
                load_coup(p, s).wait()

        for s in range(subs):
            acc[target, c, s] += nn(sol[c], coup_v[p, s])

    def rest_of_block(t):
        for delta in range(1, blocks - 1):
            valid, i, c, q = decode(t - HOP_LAG * far - SWAP_LAG - delta)

            @pl.when(valid & (q == subs - 1))
            def _():
                if delta == 1:
                    out_v[i, c] = transposed(sol[c]).astype(BF16)
                    store_out(i, c).start()

                @pl.when(i + 1 + delta < blocks)
                def _():
                    couple(i, c, i + 1 + delta)

    def flow_hi(t):
        valid, i, c, q = decode(t - HOP_LAG * z)

        @pl.when(valid & (z < last_z) & used(z + 1, x, q))
        def _():
            slot = c * subs + q
            idx = i * (chunks * subs) + slot

            @pl.when(z > 0)
            def _():
                send_hi(slot, idx).wait_recv()

            @pl.when(i > 0)
            def _():
                send_hi(slot, idx).wait_send()

            to_hi[slot] = (acc[i, c, q] + from_lo[idx].astype(F32)).astype(BF16)
            send_hi(slot, idx).start()

    def flow_lo(t):
        valid, i, c, q = decode(t - HOP_LAG * (last_z - z))

        @pl.when(valid & (z > 0))
        def _():
            slot = c * subs + q
            idx = i * (chunks * subs) + slot

            @pl.when(z < last_z)
            def _():
                send_lo(slot, idx).wait_recv()

            @pl.when(i > 0)
            def _():
                send_lo(slot, idx).wait_send()

            to_lo[slot] = (acc[i, c, q] + from_hi[idx].astype(F32)).astype(BF16)
            send_lo(slot, idx).start()

    def diagonal(t):
        valid, i, c, q = decode(t - HOP_LAG * far)

        @pl.when(valid & (q == 0))
        def _():
            prod[c] = jnp.zeros((cw, own), F32)

            @pl.when(c == 0)
            def _():
                for s in range(subs):
                    load_inv(i, s).wait()
                for s in range(chunks):
                    load_rhs(i, s).wait()

        @pl.when(valid & used(z, x, q))
        def _():
            slot = c * subs + q
            idx = i * (chunks * subs) + slot

            right = transposed(rhs_v[i, c, pl.ds(pl.multiple_of(q * qc, qc), qc), :])

            if nz > 1:
                @pl.when((z > 0) & ((z == last_z) | jnp.logical_not(used(z + 1, x, q))))
                def _():
                    send_hi(slot, idx).wait_recv()

                @pl.when(z == 0)
                def _():
                    send_lo(slot, idx).wait_recv()

            total = acc[i, c, q] + from_lo[idx].astype(F32) + from_hi[idx].astype(F32)
            residual = (right - total).astype(BF16)
            term = nt(residual, inv_v[i, q])

            prod[c] += term

            @pl.when(q == subs - 1)
            def _():
                swap_out[i, c] = prod[c].astype(BF16)
                for d in range(1, nx):
                    swap(i, c, d).start()

    def later_terms(t):
        u = t + LEAD
        c = lax.div(u, subs)
        for j in range(-(-blocks // subs)):
            i = lax.rem(u, subs) + j * subs

            @pl.when((c < chunks) & (i < blocks))
            def _():
                @pl.when(i == 0)
                def _():
                    load_later(c).wait()
                    for d in range(1, nx):
                        gather(c, d, peer(d), source(d)).wait_recv()
                    later_t[c] = transposed(later_v[c]).astype(BF16)

                @pl.when(c == 0)
                def _():
                    load_panel(i).wait()

                for s in range(subs):
                    acc[i, c, s] = nn(later_t[c], panel_v[i, :, s * qc:(s + 1) * qc])

    steps = LEAD + (blocks - 1) * period + chunks * subs + HOP_LAG * last_z + SWAP_LAG + 1

    def tick(u, carry):
        t = u - LEAD
        finish_block(t)
        flow_hi(t)
        flow_lo(t)
        diagonal(t)
        rest_of_block(t)
        later_terms(t)
        return carry

    lax.fori_loop(0, steps, tick, 0)

    for c in range(chunks):
        for d in range(1, nx):
            gather(c, d, peer(d), x).wait_send()

    @pl.when(z < last_z)
    def _():
        @pl.loop(0, chunks * subs)
        def _(slot):
            @pl.when(used(z + 1, x, lax.rem(slot, subs)))
            def _():
                send_hi(slot, slot).wait_send()

    @pl.when(z > 0)
    def _():
        @pl.loop(0, chunks * subs)
        def _(slot):
            send_lo(slot, slot).wait_send()

    for i in range(blocks):
        for c in range(chunks):
            store_out(i, c).wait()


def on_device(nz, nx, later_solution, factor_panel, coupling, inverse_diag, right_side):
    depth, blocks, bc = factor_panel.shape
    rhs_cols = later_solution.shape[1]
    pairs, own, _ = coupling.shape
    subs = max(1, min(SUBS, bc // 128))
    chunks = CHUNKS
    cw, qc = rhs_cols // chunks, bc // subs
    per_block = chunks * subs
    others = max(nx - 1, 1)
    panel = jnp.transpose(factor_panel, (1, 0, 2))
    dma = pltpu.SemaphoreType.DMA
    vmem = pltpu.VMEM
    flops = 2 * rhs_cols * bc * (depth * blocks + own * (pairs + blocks))
    return pl.pallas_call(
        functools.partial(kernel, nz, nx, chunks, subs),
        out_shape=jax.ShapeDtypeStruct((blocks, own // nx, rhs_cols), BF16),
        in_specs=[pl.BlockSpec(memory_space=pl.ANY)] * 5,
        out_specs=pl.BlockSpec(memory_space=pl.ANY),
        scratch_shapes=[
            vmem((blocks, depth, bc), BF16),
            vmem((pairs, subs, own, qc), BF16),
            vmem((blocks, subs, own, qc), BF16),
            vmem((blocks, chunks, bc, cw), BF16),
            vmem((chunks, depth, cw), BF16),
            vmem((chunks, cw, depth), BF16),
            vmem((blocks, chunks, subs, cw, qc), F32),
            vmem((blocks * per_block, cw, qc), BF16),
            vmem((blocks * per_block, cw, qc), BF16),
            vmem((per_block, cw, qc), BF16),
            vmem((per_block, cw, qc), BF16),
            vmem((chunks, cw, own), F32),
            vmem((blocks, chunks, cw, own), BF16),
            vmem((blocks, chunks, others, cw, own), BF16),
            vmem((chunks, cw, own), BF16),
            vmem((blocks, chunks, own, cw), BF16),
            dma((blocks,)), dma((pairs, subs)), dma((blocks, subs)), dma((blocks, chunks)),
            dma((chunks,)), dma((blocks, chunks)),
            dma((chunks, others)), dma((chunks, others)),
            dma((per_block,)), dma((per_block,)),
            dma((blocks * per_block,)), dma((blocks * per_block,)),
            dma((blocks, chunks, others)), dma((blocks, chunks, others)),
        ],
        compiler_params=pltpu.CompilerParams(
            collective_id=0, has_side_effects=True, vmem_limit_bytes=60 * 2**20),
        cost_estimate=pl.CostEstimate(
            flops=flops, bytes_accessed=2 * (depth * blocks * bc + own * bc * (pairs + blocks)), transcendentals=0),
    )(later_solution, panel, coupling, inverse_diag, right_side)


def solution(mesh):
    placed = (
        P(("groups", "rows", "cols"), "rhs"),
        P(("groups", "rows"), None, "cols"),
        P("groups", "rows", "cols"),
        P("groups", "rows", "cols"),
        P("groups", "cols", "rhs"),
    )
    return jax.shard_map(
        functools.partial(on_device, mesh.shape["rows"], mesh.shape["cols"]),
        mesh=mesh,
        in_specs=placed,
        out_specs=P("groups", ("rows", "cols"), "rhs"),
        check_vma=False,
    )
```
